128 devices in a mesh: row: 16 (over x_lo, z, core), col: 8 (over x_hi, y).
Axes of the slice: x: 4 (x_hi: 2, x_lo: 2; x = x_hi * 2 + x_lo), y: 4, z: 4, core: 2. Of those that a mesh axis runs over, the one named last changes fastest.
Arguments:
- basis: float32 [32768, 1024], P('row', 'col'), may hold values from -6 to 6
- merge_coef: float32 [1024, 8192], P('row', 'col'), may hold values from -0.1875 to 0.1875
- panels: float32 [2, 32768, 256], P(None, ('row', 'col')), may hold values from -0.03125 to 0.03125
- factors: float32 [2, 256, 256], replicated, may hold values from -2 to 2
Outputs:
- vectors: float32 [32768, 8192], P(('row', 'col'))
- wsum: float32 [2, 256], replicated
The draws below stay inside these ranges and needn't reach their ends.
All inputs are finite; a program needn't handle non-finite values.
Results may differ from the reference program's by a relative error of at most 0.0001.
Values sent between devices are 32-bit elements; how exact they have to be, the bound alone decides.
A program may use at most 128 MiB of HBM per device.

```python
import jax
import jax.numpy as jnp
from jax import lax

K = 1024
NB = 256
ROWS = 32768
NEV = 8192


def levels(own_key, extent, cuts, least, high):
    def one(dim, parts):
        heights = jax.random.uniform(jax.random.fold_in(jax.random.fold_in(own_key, 6), dim), (parts,), jnp.float32, least / len(cuts), high / len(cuts))
        return jnp.repeat(jnp.exp(heights), extent[dim] // parts).reshape((-1,) + (1,) * (len(extent) - dim - 1))

    level = one(*cuts[0])
    for cut in cuts[1:]:
        level = level * one(*cut)
    return level


def normal_values(rng, dims, spread, reach, pieces=(), held_as=jnp.bfloat16):
    entries = spread * jax.random.normal(rng, dims, jnp.float32)
    if pieces:
        entries = entries * levels(rng, dims, pieces, -0.22, 0.18)
    return jnp.clip(entries, -reach, reach).astype(held_as)


def setup_inputs(seed: int = 0) -> dict:
    arg_keys = jax.random.split(jax.random.key(seed), 5)
    basis = normal_values(arg_keys[0], (ROWS, K), 1.0, 6.0, ((0, 16), (1, 8)), jnp.float32)
    merge_coef = normal_values(arg_keys[1], (K, NEV), K ** -0.5, 0.1875, ((0, 16), (1, 8)), jnp.float32)
    panels = normal_values(arg_keys[2], (2, ROWS, NB), ROWS ** -0.5, 0.03125, ((1, 128),), jnp.float32)
    factors = normal_values(arg_keys[3], (2, NB, NB), (max(1, 4 * NB * NB // ROWS)) ** -0.5, 2.0, (), jnp.float32)
    return {"basis": basis, "merge_coef": merge_coef, "panels": panels, "factors": factors}


HI = lax.Precision.HIGHEST

def reference(basis, merge_coef, panels, factors):
    x = jnp.dot(basis, merge_coef, precision=HI, preferred_element_type=jnp.float32)
    totals = []
    for index in range(2):
        vecs = panels[index]
        upper = jnp.triu(factors[index])
        proj = jnp.dot(vecs.T, x, precision=HI, preferred_element_type=jnp.float32)
        totals.append(lax.optimization_barrier(jnp.sum(proj, axis=1)) / jnp.sqrt(jnp.float32(NEV)))
        scaled = jnp.dot(upper, proj, precision=HI, preferred_element_type=jnp.float32)
        x = x - jnp.dot(vecs, scaled, precision=HI, preferred_element_type=jnp.float32)
    return (x, jnp.stack(totals))
```

```python
import jax
import jax.numpy as jnp
from jax import lax
from jax.sharding import PartitionSpec as P

HI = lax.Precision.HIGHEST
MID = lax.Precision.HIGH


def matmul(left, right, precision=HI):
    return jnp.dot(left, right, precision=precision, preferred_element_type=jnp.float32)


def per_device(basis, merge_coef, panels, factors):
    tall = lax.all_to_all(basis, "col", split_axis=0, concat_axis=1, tiled=True)
    nb = panels.shape[2]
    both = jnp.concatenate([panels[0], panels[1]], axis=1)
    sums = matmul(both.T, jnp.concatenate([tall, panels[0]], axis=1))
    rows = jnp.sum(merge_coef, axis=1)
    place = lax.axis_index("row")
    line = lax.dynamic_update_slice(
        jnp.zeros((merge_coef.shape[0] * lax.axis_size("row"),), jnp.float32),
        rows, (place * merge_coef.shape[0],))
    sums, line = lax.psum((sums, line), ("row", "col"))
    coef = lax.all_gather(merge_coef, "col", axis=1, tiled=True)
    coef = lax.all_gather(coef, "row", axis=0, tiled=True)
    upper = jnp.triu(factors)
    wide = tall.shape[1]
    s0 = sums[:nb, :wide]
    s1 = sums[nb:, :wide]
    cross = sums[nb:, wide:]
    c0 = matmul(upper[0], s0)
    s1 = s1 - matmul(cross, c0)
    c1 = matmul(upper[1], s1)
    turned = tall - matmul(both, jnp.concatenate([c0, c1], axis=0))
    out = matmul(turned, coef, MID)
    scale = jnp.sqrt(jnp.float32(out.shape[1]))
    wsum = jnp.stack([jnp.sum(s0 * line, axis=1), jnp.sum(s1 * line, axis=1)]) / scale
    return out, wsum


def solution(mesh):
    return jax.shard_map(
        per_device,
        mesh=mesh,
        in_specs=(P("row", "col"), P("row", "col"), P(None, ("row", "col"), None), P()),
        out_specs=(P(("row", "col"), None), P()),
        check_vma=False,
    )
```

```python
import jax
import jax.numpy as jnp
from jax import lax
from jax.experimental import pallas as pl
from jax.experimental.pallas import tpu as pltpu
from jax.sharding import PartitionSpec as P

HI = lax.Precision.HIGHEST
MESH = pl.DeviceIdType.MESH
F32 = jnp.float32
BF16 = jnp.bfloat16

STEPS = ("a", "b", "y+", "y-", "z+", "z-")
OFFSETS = tuple((a, b, y, z) for a in (0, 1) for b in (0, 1) for y in range(4) for z in range(4))
INDEX = {d: i for i, d in enumerate(OFFSETS)}
HOME = (0, 0, 0, 0)
ROUNDS = (
    ((3, 0), (5, 0), (2, 0), (4, 0), (0, 0), (1, 0)),
    ((5, 32), (4, 32), (3, 3), (0, 16), (1, 1), (2, 32)),
    ((0, 17), (1, 35), (5, 3), (4, 33), (2, 35), (3, 35)),
    ((0, 51), (4, 49), (5, 4), (1, 2), (2, 34), (3, 1)),
    ((0, 38), (5, 38), (4, 4), (1, 4), (3, 2), (2, 36)),
    ((4, 47), (5, 47), (0, 13), (1, 5), (3, 15), (2, 37)),
    ((5, 40), (4, 11), (0, 41), (2, 6), (3, 46), (1, 36)),
    ((0, 21), (4, 21), (5, 52), (3, 19), (2, 50), (1, 7)),
    ((0, 31), (5, 31), (4, 31), (3, 48), (2, 52), (1, 13)),
    ((5, 63), (4, 60), (0, 56), (3, 63), (2, 21), (1, 10)),
    ((4, 26), (5, 59), (3, 61)),
)
HALVES = 2


def onward(d, step):
    a, b, y, z = d
    if step == "a":
        return 1 - a, b, y, z
    if step == "b":
        return a, 1 - b, y, z
    if step in ("y+", "y-"):
        return a, b, (y + (1 if step == "y+" else 3)) % 4, z
    return a, b, y, (z + (1 if step == "z+" else 3)) % 4


PLAN = tuple(
    tuple((STEPS[s], OFFSETS[i], onward(OFFSETS[i], STEPS[s])) for s, i in line) for line in ROUNDS
)


def coords(row, col):
    return row // 8, (row // 2) % 4, row % 2, col // 4, col % 4


def place(xl, z, k, xh, y):
    return xl * 8 + z * 2 + k, xh * 4 + y


def neighbour(row, col, step):
    xl, z, k, xh, y = coords(row, col)
    if step == "a":
        xl = 1 - xl
    elif step == "b":
        xl, xh = 1 - xl, 1 - xh
    elif step == "y+":
        y = (y + 1) % 4
    elif step == "y-":
        y = (y + 3) % 4
    elif step == "z+":
        z = (z + 1) % 4
    elif step == "z-":
        z = (z + 3) % 4
    else:
        k = 1 - k
    return place(xl, z, k, xh, y)


def source(row, col, d, other=0):
    xl, z, k, xh, y = coords(row, col)
    a, b, dy, dz = d
    return place(
        (xl + a + b) % 2, (z + 4 - dz) % 4, (k + other) % 2, (xh + b) % 2, (y + 4 - dy) % 4
    )


def group(d):
    return d[1], d[2]


def group_order():
    last = {}
    for t, line in enumerate(PLAN):
        for _, _, n in line:
            last[group(n)] = t
    return sorted(last.items(), key=lambda kv: kv[1])


def split(x):
    high = x.astype(BF16)
    return high, (x - high.astype(F32)).astype(BF16)


def kernel(
    m_ref, turned_ref, out_ref, line_ref,
    full, parts, made, recv, sent, krecv, ksent, local, outsem,
):
    row = lax.axis_index("row")
    col = lax.axis_index("col")
    depth = m_ref.shape[0]
    piece = depth // HALVES
    tile = 256
    tiles = full.shape[2] // tile
    peer = {step: neighbour(row, col, step) for step in STEPS + ("k",)}

    barrier = pltpu.get_barrier_semaphore()
    for step in STEPS + ("k",):
        pl.semaphore_signal(barrier, inc=1, device_id=peer[step], device_id_type=MESH)
    pl.semaphore_wait(barrier, len(peer))

    def slot(d, other=0, half=None):
        r, c = source(row, col, d, other)
        if half is None:
            return full.at[c, pl.ds(pl.multiple_of(r * depth, depth), depth), :]
        return full.at[c, pl.ds(pl.multiple_of(r * depth + half * piece, piece), piece), :]

    def held(d, half=None):
        if d == HOME:
            return m_ref if half is None else m_ref.at[pl.ds(half * piece, piece), :]
        return slot(d, 0, half)

    def send(step, d, n, half):
        copy = pltpu.make_async_remote_copy(
            held(d, half), slot(d, 0, half), sent.at[INDEX[n], half], recv.at[INDEX[n], half],
            peer[step], device_id_type=MESH)
        copy.start()
        return copy

    def arrive(n, half):
        pltpu.make_async_remote_copy(
            slot(n, 0, half), slot(n, 0, half), sent.at[INDEX[n], half], recv.at[INDEX[n], half],
            peer["k"], device_id_type=MESH).wait_recv()

    def share(d):
        copy = pltpu.make_async_remote_copy(
            held(d), slot(d), ksent.at[INDEX[d]], krecv.at[INDEX[d]],
            peer["k"], device_id_type=MESH)
        copy.start()
        return copy

    def shared(d):
        pltpu.make_async_remote_copy(
            slot(d, 1), slot(d, 1), ksent.at[INDEX[d]], krecv.at[INDEX[d]],
            peer["k"], device_id_type=MESH).wait_recv()

    own = pltpu.make_async_copy(m_ref, slot(HOME), local)
    own.start()
    started = []
    stores = []
    arrived = set()
    todo = []
    order = group_order()

    def compute(g, first, count):
        b, dy = g
        _, c = source(row, col, (0, b, dy, 0))
        q = [name for name, _ in order].index(g)
        if first == 0:
            for d in OFFSETS:
                if group(d) == g:
                    shared(d)
            if g == group(HOME):
                own.wait()

        def unit(n, carry):
            at = pl.ds(pl.multiple_of(n * tile, tile), tile)
            m = full[c, :, at]
            high, low = split(m)
            both = jnp.dot(parts[...], high, preferred_element_type=F32)
            rest = jnp.dot(parts[: both.shape[0] // 2, :], low, preferred_element_type=F32)
            half = both.shape[0] // 2
            made[q, :, at] = both[:half] + (both[half:] + rest)
            line_ref[...] += m[:, :128] + m[:, 128:]
            return carry

        lax.fori_loop(first, first + count, unit, 0)
        if first + count == tiles:
            wide = made.shape[2]
            store = pltpu.make_async_copy(
                made.at[q], out_ref.at[:, pl.ds(pl.multiple_of(c * wide, wide), wide)],
                outsem.at[q])
            store.start()
            stores.append(store)

    def some(count):
        while count and todo:
            g, first = todo.pop(0)
            take = min(count, tiles - first)
            compute(g, first, take)
            count -= take
            if first + take < tiles:
                todo.insert(0, (g, first + take))

    for t, plan in enumerate(PLAN):
        for half in range(HALVES):
            for step, d, n in plan:
                if d != HOME and (d, half) not in arrived:
                    arrive(d, half)
                    arrived.add((d, half))
                started.append(send(step, d, n, half))
            if t == 0 and half == 0:
                started.append(share(HOME))
                high, low = split(turned_ref[...])
                rows = turned_ref.shape[0]
                parts[:rows, :] = high
                parts[rows:, :] = low
                line_ref[...] = jnp.zeros_like(line_ref)
            some(2)
        if t:
            for _, _, n in PLAN[t - 1]:
                for half in range(HALVES):
                    if (n, half) not in arrived:
                        arrive(n, half)
                        arrived.add((n, half))
                started.append(share(n))
        todo.extend((g, 0) for g, last in order if last == t - 1)
    for _, _, n in PLAN[-1]:
        for half in range(HALVES):
            arrive(n, half)
        started.append(share(n))
    todo.extend((g, 0) for g, last in order if last == len(PLAN) - 1)
    some(len(order) * tiles)
    for copy in started:
        copy.wait_send()
    for copy in stores:
        copy.wait()


def gathered_product(turned, merge_coef, cols):
    rows, inner = turned.shape
    depth, wide = merge_coef.shape
    groups = cols // wide
    sems = pltpu.SemaphoreType.DMA
    return pl.pallas_call(
        kernel,
        out_shape=(
            jax.ShapeDtypeStruct((rows, cols), F32),
            jax.ShapeDtypeStruct((inner, 128), F32),
        ),
        in_specs=[pl.BlockSpec(memory_space=pltpu.VMEM)] * 2,
        out_specs=(pl.BlockSpec(memory_space=pl.ANY), pl.BlockSpec(memory_space=pltpu.VMEM)),
        scratch_shapes=[
            pltpu.VMEM((groups, inner, wide), F32),
            pltpu.VMEM((2 * rows, inner), BF16),
            pltpu.VMEM((groups, rows, wide), F32),
            sems((len(OFFSETS), HALVES)),
            sems((len(OFFSETS), HALVES)),
            sems((len(OFFSETS),)),
            sems((len(OFFSETS),)),
            sems,
            sems((groups,)),
        ],
        compiler_params=pltpu.CompilerParams(
            collective_id=0, has_side_effects=True, vmem_limit_bytes=58 * 2**20
        ),
        cost_estimate=pl.CostEstimate(
            flops=6 * rows * inner * cols, bytes_accessed=4 * rows * cols, transcendentals=0
        ),
    )(merge_coef, turned)


def matmul(left, right, precision=HI):
    return jnp.dot(left, right, precision=precision, preferred_element_type=F32)


def per_device(basis, merge_coef, panels, factors):
    tall = lax.all_to_all(basis, "col", split_axis=0, concat_axis=1, tiled=True)
    nb = panels.shape[2]
    both = jnp.concatenate([panels[0], panels[1]], axis=1)
    sums = matmul(both.T, jnp.concatenate([tall, panels[0]], axis=1))
    sums = lax.psum(sums, ("row", "col"))
    upper = jnp.triu(factors)
    wide = tall.shape[1]
    s0 = sums[:nb, :wide]
    s1 = sums[nb:, :wide]
    cross = sums[nb:, wide:]
    c0 = matmul(upper[0], s0)
    s1 = s1 - matmul(cross, c0)
    c1 = matmul(upper[1], s1)
    turned = tall - matmul(both, jnp.concatenate([c0, c1], axis=0))
    cols = merge_coef.shape[1] * lax.axis_size("col")
    out, lanes = gathered_product(turned, merge_coef, cols)
    line = jnp.sum(lanes, axis=1)
    wsum = jnp.stack([jnp.sum(s0 * line, axis=1), jnp.sum(s1 * line, axis=1)])
    return out, wsum / jnp.sqrt(F32(cols))


def solution(mesh):
    return jax.shard_map(
        per_device,
        mesh=mesh,
        in_specs=(P("row", "col"), P("row", "col"), P(None, ("row", "col"), None), P()),
        out_specs=(P(("row", "col"), None), P()),
        check_vma=False,
    )
```

```python
import jax
import jax.numpy as jnp
from jax import lax
from jax.experimental import pallas as pl
from jax.experimental.pallas import tpu as pltpu
from jax.sharding import PartitionSpec as P

HI = lax.Precision.HIGHEST
MESH = pl.DeviceIdType.MESH
F32 = jnp.float32
BF16 = jnp.bfloat16

STEPS = ("a", "b", "y+", "y-", "z+", "z-")
OFFSETS = tuple((a, b, y, z) for a in (0, 1) for b in (0, 1) for y in range(4) for z in range(4))
INDEX = {d: i for i, d in enumerate(OFFSETS)}
HOME = (0, 0, 0, 0)
ROUNDS = (
    ((3, 0), (5, 0), (2, 0), (4, 0), (0, 0), (1, 0)),
    ((5, 32), (4, 32), (3, 3), (0, 16), (1, 1), (2, 32)),
    ((0, 17), (1, 35), (5, 3), (4, 33), (2, 35), (3, 35)),
    ((0, 51), (4, 49), (5, 4), (1, 2), (2, 34), (3, 1)),
    ((0, 38), (5, 38), (4, 4), (1, 4), (3, 2), (2, 36)),
    ((4, 47), (5, 47), (0, 13), (1, 5), (3, 15), (2, 37)),
    ((5, 40), (4, 11), (0, 41), (2, 6), (3, 46), (1, 36)),
    ((0, 21), (4, 21), (5, 52), (3, 19), (2, 50), (1, 7)),
    ((0, 31), (5, 31), (4, 31), (3, 48), (2, 52), (1, 13)),
    ((5, 63), (4, 60), (0, 56), (3, 63), (2, 21), (1, 10)),
    ((4, 26), (5, 59), (3, 61)),
)
HALVES = 2


def onward(d, step):
    a, b, y, z = d
    if step == "a":
        return 1 - a, b, y, z
    if step == "b":
        return a, 1 - b, y, z
    if step in ("y+", "y-"):
        return a, b, (y + (1 if step == "y+" else 3)) % 4, z
    return a, b, y, (z + (1 if step == "z+" else 3)) % 4


PLAN = tuple(
    tuple((STEPS[s], OFFSETS[i], onward(OFFSETS[i], STEPS[s])) for s, i in line) for line in ROUNDS
)


def coords(row, col):
    return row // 8, (row // 2) % 4, row % 2, col // 4, col % 4


def place(xl, z, k, xh, y):
    return xl * 8 + z * 2 + k, xh * 4 + y


def neighbour(row, col, step):
    xl, z, k, xh, y = coords(row, col)
    if step == "a":
        xl = 1 - xl
    elif step == "b":
        xl, xh = 1 - xl, 1 - xh
    elif step == "y+":
        y = (y + 1) % 4
    elif step == "y-":
        y = (y + 3) % 4
    elif step == "z+":
        z = (z + 1) % 4
    elif step == "z-":
        z = (z + 3) % 4
    else:
        k = 1 - k
    return place(xl, z, k, xh, y)


def source(row, col, d, other=0):
    xl, z, k, xh, y = coords(row, col)
    a, b, dy, dz = d
    return place(
        (xl + a + b) % 2, (z + 4 - dz) % 4, (k + other) % 2, (xh + b) % 2, (y + 4 - dy) % 4
    )


def group(d):
    return d[1], d[2]


def group_order():
    last = {}
    for t, line in enumerate(PLAN):
        for _, _, n in line:
            last[group(n)] = t
    return sorted(last.items(), key=lambda kv: kv[1])


def split(x):
    high = x.astype(BF16)
    return high, (x - high.astype(F32)).astype(BF16)


def dot(left, right, precision=HI):
    return jnp.dot(left, right, precision=precision, preferred_element_type=F32)


AXES = (("z", "y", "x"), ("y", "x", "z"), ("x", "z", "y"))
TICKS = (5, 6, 8, 9, 11, 12, 13, 15)
BATCH = 5


def along(row, col, axis, step):
    xl, z, k, xh, y = coords(row, col)
    if axis == "x":
        x = (xh * 2 + xl + step) % 4
        xl, xh = x % 2, x // 2
    elif axis == "y":
        y = (y + step) % 4
    else:
        z = (z + step) % 4
    return place(xl, z, k, xh, y)


def position(row, col, axis):
    xl, z, _, xh, y = coords(row, col)
    return {"x": xh * 2 + xl, "y": y, "z": z}[axis]


def kernel(
    m_ref, basis_ref, panel_ref, factor_ref, out_ref, wsum_ref,
    full, parts, made, line, tall, mine, twin, paired, near, nearest, mid, middle, far, total, proj,
    recv, sent, krecv, ksent, local, outsem, trecv, tsent, rrecv, rsent,
):
    row = lax.axis_index("row")
    col = lax.axis_index("col")
    _, _, core, _, _ = coords(row, col)
    depth = m_ref.shape[0]
    piece = depth // HALVES
    tile = 256
    tiles = full.shape[2] // tile
    groups = full.shape[0]
    rows = made.shape[1]
    nb = panel_ref.shape[2]
    peer = {step: neighbour(row, col, step) for step in STEPS + ("k",)}

    barrier = pltpu.get_barrier_semaphore()
    greeted = [(row, (col + o) % groups) for o in range(1, groups)]
    greeted += [along(row, col, "x", o) for o in (1, 3)]
    greeted += [along(row, col, "z", o) for o in (1, 2, 3)]
    greeted += [peer["k"]]
    for device in greeted:
        pl.semaphore_signal(barrier, inc=1, device_id=device, device_id_type=MESH)
    pl.semaphore_wait(barrier, len(greeted))

    started = []
    stores = []
    arrived = set()
    todo = []
    order = group_order()

    def remote(src, dst, out_sem, in_sem, device, start=True):
        copy = pltpu.make_async_remote_copy(
            src, dst, out_sem, in_sem, device, device_id_type=MESH)
        if start:
            copy.start()
            started.append(copy)
        return copy


    def slot(d, other=0, half=None):
        r, c = source(row, col, d, other)
        if half is None:
            return full.at[c, pl.ds(pl.multiple_of(r * depth, depth), depth), :]
        return full.at[c, pl.ds(pl.multiple_of(r * depth + half * piece, piece), piece), :]

    def held(d, half=None):
        if d == HOME:
            return m_ref if half is None else m_ref.at[pl.ds(half * piece, piece), :]
        return slot(d, 0, half)

    def send(step, d, n, half):
        i = INDEX[n]
        remote(held(d, half), slot(d, 0, half), sent.at[i, half], recv.at[i, half], peer[step])

    def arrive(n, half):
        if (n, half) in arrived or n == HOME:
            return
        arrived.add((n, half))
        i, here = INDEX[n], slot(n, 0, half)
        remote(here, here, sent.at[i, half], recv.at[i, half], peer["k"], False).wait_recv()

    def share(d):
        remote(held(d), slot(d), ksent.at[INDEX[d]], krecv.at[INDEX[d]], peer["k"])

    def shared(d):
        i, here = INDEX[d], slot(d, 1)
        remote(here, here, ksent.at[i], krecv.at[i], peer["k"], False).wait_recv()


    def block(j):
        return basis_ref.at[pl.ds(pl.multiple_of(j * rows, rows), rows), :]

    own_tall = pltpu.make_async_copy(block(col), tall.at[col], local.at[1])

    def spread():
        own_tall.start()
        for o in range(1, groups):
            j = (col + o) % groups
            remote(block(j), tall.at[col], tsent.at[o - 1], trecv.at[o - 1], (row, j))


    wide = total.shape[2]
    per = wide // 128

    def partial():
        turned = jnp.transpose(jnp.concatenate([panel_ref[0], panel_ref[1]], axis=1))
        cross = dot(turned[nb:], panel_ref[0])
        last = len(AXES) - 1
        mine[last, :nb, wide - 128 :] = cross[:, :128]
        mine[last, nb:, wide - 128 :] = cross[:, 128:]
        own_tall.wait()
        for o in range(1, groups):
            here = tall.at[(col + groups - o) % groups]
            remote(here, here, tsent.at[o - 1], trecv.at[o - 1], peer["k"], False).wait_recv()
        for p in range(len(AXES)):
            count = min(per, groups - p * per)
            value = jnp.concatenate([tall[p * per + i] for i in range(count)], axis=1)
            mine[p, :, : count * 128] = dot(turned, value)
            other = pl.ds(pl.multiple_of((1 - core) * nb, nb), nb)
            remote(mine.at[p, other], twin.at[p], rsent.at[p, 0], rrecv.at[p, 0], peer["k"])

    def exchange(p, level, src_of, dst_of):
        axis = AXES[p][(0, 1, 2, 1, 0)[level]]
        for o in (1, 2, 3):
            j = (position(row, col, axis) + o) % 4
            at = 1 + level * 3 + o - 1
            remote(src_of(j), dst_of(o), rsent.at[p, at], rrecv.at[p, at],
                   along(row, col, axis, o))

    def exchanged(p, level, dst_of):
        for o in (1, 2, 3):
            at = 1 + level * 3 + o - 1
            here = dst_of(o)
            remote(here, here, rsent.at[p, at], rrecv.at[p, at], peer["k"], False).wait_recv()

    def pos(p, level):
        return position(row, col, AXES[p][level])

    def cut(ref, p, j, size):
        return ref.at[p, pl.ds(pl.multiple_of(j * size, size), size), :]

    first, second = nb // 4, nb // 16

    def pair():
        for p in range(len(AXES)):
            remote(twin.at[p], twin.at[p], rsent.at[p, 0], rrecv.at[p, 0], peer["k"],
                   False).wait_recv()
            keep = pl.ds(pl.multiple_of(core * nb, nb), nb)
            paired[p] = mine[p, keep, :] + twin[p]
            exchange(p, 0, lambda j: cut(paired, p, j, first), lambda o: near.at[p, o - 1])

    def level_one():
        for p in range(len(AXES)):
            exchanged(p, 0, lambda o: near.at[p, o - 1])
            keep = pl.ds(pl.multiple_of(pos(p, 0) * first, first), first)
            nearest[p] = (paired[p, keep, :] + near[p, 0]) + (near[p, 1] + near[p, 2])
            exchange(p, 1, lambda j: cut(nearest, p, j, second), lambda o: mid.at[p, o - 1])

    def level_two():
        for p in range(len(AXES)):
            exchanged(p, 1, lambda o: mid.at[p, o - 1])
            keep = pl.ds(pl.multiple_of(pos(p, 1) * second, second), second)
            value = (nearest[p, keep, :] + mid[p, 0]) + (mid[p, 1] + mid[p, 2])
            middle[p] = value
            far[p, pos(p, 2)] = value
            here = pos(p, 2)
            exchange(p, 2, lambda j: middle.at[p], lambda o: far.at[p, here])

    def level_three():
        for p in range(len(AXES)):
            here = pos(p, 2)
            exchanged(p, 2, lambda o: far.at[p, (here + 4 - o) % 4])
            at = core * nb + pos(p, 0) * first + pos(p, 1) * second
            strip = pl.ds(pl.multiple_of(at, second), second)
            total[p, strip, :] = (far[p, 0] + far[p, 1]) + (far[p, 2] + far[p, 3])
            own = total.at[p, strip, :]
            exchange(p, 3, lambda j: own, lambda o: own)

    def strip_of(p, level, o):
        one = (pos(p, 0) + (4 - o if level == 4 else 0)) % 4
        if level == 4:
            return total.at[
                p, pl.ds(pl.multiple_of(core * nb + one * first, first), first), :]
        two = (pos(p, 1) + 4 - o) % 4
        at = core * nb + one * first + two * second
        return total.at[p, pl.ds(pl.multiple_of(at, second), second), :]

    def gather_one():
        for p in range(len(AXES)):
            exchanged(p, 3, lambda o: strip_of(p, 3, o))
            own = strip_of(p, 4, 0)
            exchange(p, 4, lambda j: own, lambda o: own)

    def gather_two():
        for p in range(len(AXES)):
            exchanged(p, 4, lambda o: strip_of(p, 4, o))
            own = cut(total, p, core, nb)
            remote(own, own, rsent.at[p, 16], rrecv.at[p, 16], peer["k"])

    def turn():
        for p in range(len(AXES)):
            here = cut(total, p, 1 - core, nb)
            remote(here, here, rsent.at[p, 16], rrecv.at[p, 16], peer["k"], False).wait_recv()
        last = len(AXES) - 1
        cross = jnp.concatenate(
            [total[last, :nb, wide - 128 :], total[last, nb:, wide - 128 :]], axis=1)
        keep = lax.broadcasted_iota(jnp.int32, (nb, nb), 0) <= lax.broadcasted_iota(
            jnp.int32, (nb, nb), 1)
        one = jnp.where(keep, factor_ref[0], 0.0)
        two = jnp.where(keep, factor_ref[1], 0.0)
        for p in range(len(AXES)):
            count = min(per, groups - p * per)
            at = pl.ds(p * wide, count * 128)
            s0 = total[p, :nb, : count * 128]
            c0 = dot(one, s0)
            s1 = total[p, nb:, : count * 128] - dot(cross, c0)
            c1 = dot(two, s1)
            proj[:nb, at] = s0
            proj[nb:, at] = s1
            value = jnp.concatenate([tall[p * per + i] for i in range(count)], axis=1)
            value = value - (dot(panel_ref[0], c0) + dot(panel_ref[1], c1))
            high, low = split(value)
            parts[:rows, at] = high
            parts[rows:, at] = low


    own = pltpu.make_async_copy(m_ref, slot(HOME), local.at[0])

    def compute(g, begin, count):
        b, dy = g
        _, c = source(row, col, (0, b, dy, 0))
        q = [name for name, _ in order].index(g)
        if begin == 0:
            for d in OFFSETS:
                if group(d) == g:
                    shared(d)
            if g == group(HOME):
                own.wait()
            if q >= made.shape[0]:
                stores[q - made.shape[0]].wait()
        where = q % made.shape[0]

        def unit(n, carry):
            at = pl.ds(pl.multiple_of(n * tile, tile), tile)
            m = full[c, :, at]
            high, low = split(m)
            both = jnp.dot(parts[...], high, preferred_element_type=F32)
            rest = jnp.dot(parts[:rows, :], low, preferred_element_type=F32)
            made[where, :, at] = both[:rows] + (both[rows:] + rest)
            line[...] += m[:, :128] + m[:, 128:]
            return carry

        lax.fori_loop(begin, begin + count, unit, 0)
        if begin + count == tiles:
            span = made.shape[2]
            store = pltpu.make_async_copy(
                made.at[where], out_ref.at[:, pl.ds(pl.multiple_of(c * span, span), span)],
                outsem.at[q])
            store.start()
            stores.append(store)

    def some(count):
        while count and todo:
            g, begin = todo.pop(0)
            take = min(count, tiles - begin)
            compute(g, begin, take)
            count -= take
            if begin + take < tiles:
                todo.insert(0, (g, begin + take))

    spread()
    own.start()
    line[...] = jnp.zeros_like(line)
    steps = [partial, pair, level_one, level_two, level_three, gather_one, gather_two, turn]
    tick = 0
    for t, plan in enumerate(PLAN):
        for half in range(HALVES):
            for step, d, n in plan:
                arrive(d, half)
                send(step, d, n, half)
            if t == 0 and half == 0:
                share(HOME)
            for at, action in zip(TICKS, steps):
                if at == tick:
                    action()
            if tick >= TICKS[-1]:
                some(BATCH)
            tick += 1
        if t:
            for _, _, n in PLAN[t - 1]:
                for half in range(HALVES):
                    arrive(n, half)
                share(n)
        todo.extend((g, 0) for g, last in order if last == t - 1)
    for _, _, n in PLAN[-1]:
        for half in range(HALVES):
            arrive(n, half)
        share(n)
    todo.extend((g, 0) for g, last in order if last == len(PLAN) - 1)
    some(len(order) * tiles)
    lanes = jnp.transpose(dot(proj[...], line[...]))
    sums = jnp.sum(lanes, axis=0, keepdims=True) / jnp.sqrt(F32(groups * full.shape[2]))
    wsum_ref[0:1, :] = sums[:, :nb]
    wsum_ref[1:2, :] = sums[:, nb:]
    for copy in started:
        copy.wait_send()
    for copy in stores[-made.shape[0] :]:
        copy.wait()


def per_device(basis, merge_coef, panels, factors):
    depth, span = merge_coef.shape
    groups = lax.axis_size("col")
    rows = basis.shape[0] // groups
    inner = basis.shape[1] * groups
    cols = span * groups
    nb = panels.shape[2]
    wide = (groups // len(AXES) + 1) * 128
    sems = pltpu.SemaphoreType.DMA
    vmem = lambda *shape: pltpu.VMEM(shape, F32)
    n = len(AXES)
    return pl.pallas_call(
        kernel,
        out_shape=(
            jax.ShapeDtypeStruct((rows, cols), F32),
            jax.ShapeDtypeStruct((2, nb), F32),
        ),
        in_specs=[pl.BlockSpec(memory_space=pltpu.VMEM)] * 4,
        out_specs=(pl.BlockSpec(memory_space=pl.ANY), pl.BlockSpec(memory_space=pltpu.VMEM)),
        scratch_shapes=[
            vmem(groups, inner, span),
            pltpu.VMEM((2 * rows, inner), BF16),
            vmem(groups // 2, rows, span),
            vmem(inner, 128),
            vmem(groups, rows, 128),
            vmem(n, 2 * nb, wide),
            vmem(n, nb, wide),
            vmem(n, nb, wide),
            vmem(n, 3, nb // 4, wide),
            vmem(n, nb // 4, wide),
            vmem(n, 3, nb // 16, wide),
            vmem(n, nb // 16, wide),
            vmem(n, 4, nb // 16, wide),
            vmem(n, 2 * nb, wide),
            vmem(2 * nb, inner),
            sems((len(OFFSETS), HALVES)),
            sems((len(OFFSETS), HALVES)),
            sems((len(OFFSETS),)),
            sems((len(OFFSETS),)),
            sems((2,)),
            sems((groups,)),
            sems((groups - 1,)),
            sems((groups - 1,)),
            sems((n, 17)),
            sems((n, 17)),
        ],
        compiler_params=pltpu.CompilerParams(
            collective_id=0, has_side_effects=True, vmem_limit_bytes=60 * 2**20
        ),
        cost_estimate=pl.CostEstimate(
            flops=6 * rows * inner * cols, bytes_accessed=4 * rows * cols, transcendentals=0
        ),
    )(merge_coef, basis, panels, factors)


def solution(mesh):
    return jax.shard_map(
        per_device,
        mesh=mesh,
        in_specs=(P("row", "col"), P("row", "col"), P(None, ("row", "col"), None), P()),
        out_specs=(P(("row", "col"), None), P()),
        check_vma=False,
    )
```

```python
import functools

import jax
import jax.numpy as jnp
from jax import lax
from jax.experimental import pallas as pl
from jax.experimental.pallas import tpu as pltpu
from jax.sharding import PartitionSpec as P

HI = lax.Precision.HIGHEST
MESH = pl.DeviceIdType.MESH
F32 = jnp.float32
BF16 = jnp.bfloat16

STEPS = ("a", "b", "y+", "y-", "z+", "z-")
OFFSETS = tuple((a, b, y, z) for a in (0, 1) for b in (0, 1) for y in range(4) for z in range(4))
INDEX = {d: i for i, d in enumerate(OFFSETS)}
HOME = (0, 0, 0, 0)
ROUNDS = (
    ((3, 0), (5, 0), (2, 0), (4, 0), (0, 0), (1, 0)),
    ((5, 32), (4, 32), (3, 3), (0, 16), (1, 1), (2, 32)),
    ((0, 17), (1, 35), (5, 3), (4, 33), (2, 35), (3, 35)),
    ((0, 51), (4, 49), (5, 4), (1, 2), (2, 34), (3, 1)),
    ((0, 38), (5, 38), (4, 4), (1, 4), (3, 2), (2, 36)),
    ((4, 47), (5, 47), (0, 13), (1, 5), (3, 15), (2, 37)),
    ((5, 40), (4, 11), (0, 41), (2, 6), (3, 46), (1, 36)),
    ((0, 21), (4, 21), (5, 52), (3, 19), (2, 50), (1, 7)),
    ((0, 31), (5, 31), (4, 31), (3, 48), (2, 52), (1, 13)),
    ((5, 63), (4, 60), (0, 56), (3, 63), (2, 21), (1, 10)),
    ((4, 26), (5, 59), (3, 61)),
)
HALVES = 4


def onward(d, step):
    a, b, y, z = d
    if step == "a":
        return 1 - a, b, y, z
    if step == "b":
        return a, 1 - b, y, z
    if step in ("y+", "y-"):
        return a, b, (y + (1 if step == "y+" else 3)) % 4, z
    return a, b, y, (z + (1 if step == "z+" else 3)) % 4


PLAN = tuple(
    tuple((STEPS[s], OFFSETS[i], onward(OFFSETS[i], STEPS[s])) for s, i in line) for line in ROUNDS
)


def coords(row, col):
    return row // 8, (row // 2) % 4, row % 2, col // 4, col % 4


def place(xl, z, k, xh, y):
    return xl * 8 + z * 2 + k, xh * 4 + y


def neighbour(row, col, step):
    xl, z, k, xh, y = coords(row, col)
    if step == "a":
        xl = 1 - xl
    elif step == "b":
        xl, xh = 1 - xl, 1 - xh
    elif step == "y+":
        y = (y + 1) % 4
    elif step == "y-":
        y = (y + 3) % 4
    elif step == "z+":
        z = (z + 1) % 4
    elif step == "z-":
        z = (z + 3) % 4
    else:
        k = 1 - k
    return place(xl, z, k, xh, y)


def source(row, col, d, other=0):
    xl, z, k, xh, y = coords(row, col)
    a, b, dy, dz = d
    return place(
        (xl + a + b) % 2, (z + 4 - dz) % 4, (k + other) % 2, (xh + b) % 2, (y + 4 - dy) % 4
    )


def group(d):
    return d[1], d[2]


def group_order():
    last = {}
    for t, line in enumerate(PLAN):
        for _, _, n in line:
            last[group(n)] = t
    return sorted(last.items(), key=lambda kv: kv[1])


def split(x):
    high = x.astype(BF16)
    return high, (x - high.astype(F32)).astype(BF16)


def dot(left, right, precision=HI):
    return jnp.dot(left, right, precision=precision, preferred_element_type=F32)


def dot3(left, right):
    (a, b), (c, d) = split(left), split(right)
    part = functools.partial(jnp.dot, preferred_element_type=F32)
    return part(a, c) + (part(a, d) + part(b, c))


AXES = (("z", "y", "x"), ("y", "x", "z"), ("x", "z", "y"))
TICKS = (8, 8, 10, 14, 17, 20, 23, 26, 30)
BATCH = 1


def along(row, col, axis, step):
    xl, z, k, xh, y = coords(row, col)
    if axis == "x":
        x = (xh * 2 + xl + step) % 4
        xl, xh = x % 2, x // 2
    elif axis == "y":
        y = (y + step) % 4
    else:
        z = (z + step) % 4
    return place(xl, z, k, xh, y)


def position(row, col, axis):
    xl, z, _, xh, y = coords(row, col)
    return {"x": xh * 2 + xl, "y": y, "z": z}[axis]


def kernel(
    m_ref, basis_ref, panel_ref, factor_ref, out_ref, wsum_ref,
    full, parts, line, turned, tall, mine, twin, paired, near, nearest, mid, middle, far, total, proj,
    recv, sent, krecv, ksent, local, outsem, trecv, tsent, rrecv, rsent,
):
    row = lax.axis_index("row")
    col = lax.axis_index("col")
    _, _, core, _, _ = coords(row, col)
    depth = m_ref.shape[0]
    piece = depth // HALVES
    tile = 512
    tiles = full.shape[2] // tile
    groups = full.shape[0]
    rows = out_ref.shape[0]
    nb = panel_ref.shape[2]
    peer = {step: neighbour(row, col, step) for step in STEPS + ("k",)}

    barrier = pltpu.get_barrier_semaphore()
    greeted = [(row, (col + o) % groups) for o in range(1, groups)]
    greeted += [along(row, col, "x", o) for o in (1, 3)]
    greeted += [along(row, col, "z", o) for o in (1, 2, 3)]
    greeted += [peer["k"]]
    for device in greeted:
        pl.semaphore_signal(barrier, inc=1, device_id=device, device_id_type=MESH)
    started = []
    stores = []
    arrived = set()
    todo = []
    order = group_order()

    def remote(src, dst, out_sem, in_sem, device, start=True):
        copy = pltpu.make_async_remote_copy(
            src, dst, out_sem, in_sem, device, device_id_type=MESH)
        if start:
            copy.start()
            started.append(copy)
        return copy


    def slot(d, other=0, half=None):
        r, c = source(row, col, d, other)
        if half is None:
            return full.at[c, pl.ds(pl.multiple_of(r * depth, depth), depth), :]
        return full.at[c, pl.ds(pl.multiple_of(r * depth + half * piece, piece), piece), :]

    def held(d, half=None):
        if d == HOME:
            return m_ref if half is None else m_ref.at[pl.ds(half * piece, piece), :]
        return slot(d, 0, half)

    def send(step, d, n, half):
        i = INDEX[n]
        remote(held(d, half), slot(d, 0, half), sent.at[i, half], recv.at[i, half], peer[step])

    def arrive(n, half):
        if (n, half) in arrived or n == HOME:
            return
        arrived.add((n, half))
        i, here = INDEX[n], slot(n, 0, half)
        remote(here, here, sent.at[i, half], recv.at[i, half], peer["k"], False).wait_recv()

    def share(d):
        remote(held(d), slot(d), ksent.at[INDEX[d]], krecv.at[INDEX[d]], peer["k"])

    def shared(d):
        i, here = INDEX[d], slot(d, 1)
        remote(here, here, ksent.at[i], krecv.at[i], peer["k"], False).wait_recv()


    def block(j):
        return basis_ref.at[pl.ds(pl.multiple_of(j * rows, rows), rows), :]

    own_tall = pltpu.make_async_copy(block(col), tall.at[col], local.at[1])

    def spread():
        for o in range(1, groups):
            j = (col + o) % groups
            remote(block(j), tall.at[col], tsent.at[o - 1], trecv.at[o - 1], (row, j))


    wide = total.shape[2]
    per = wide // 128

    def begin():
        value = jnp.transpose(jnp.concatenate([panel_ref[0], panel_ref[1]], axis=1))
        turned[...] = value
        cross = dot3(value[nb:], panel_ref[0])
        last = len(AXES) - 1
        mine[last, :nb, wide - 128 :] = cross[:, :128]
        mine[last, nb:, wide - 128 :] = cross[:, 128:]

    def landed():
        own_tall.wait()
        for o in range(1, groups):
            here = tall.at[(col + groups - o) % groups]
            remote(here, here, tsent.at[o - 1], trecv.at[o - 1], peer["k"], False).wait_recv()

    def partial():
        for p in range(len(AXES)):
            count = min(per, groups - p * per)
            value = jnp.concatenate([tall[p * per + i] for i in range(count)], axis=1)
            mine[p, :, : count * 128] = dot3(turned[...], value)
            other = pl.ds(pl.multiple_of((1 - core) * nb, nb), nb)
            remote(mine.at[p, other], twin.at[p], rsent.at[p, 0], rrecv.at[p, 0], peer["k"])

    def exchange(p, level, src_of, dst_of):
        axis = AXES[p][(0, 1, 2, 1, 0)[level]]
        for o in (1, 2, 3):
            j = (position(row, col, axis) + o) % 4
            at = 1 + level * 3 + o - 1
            remote(src_of(j), dst_of(o), rsent.at[p, at], rrecv.at[p, at],
                   along(row, col, axis, o))

    def exchanged(p, level, dst_of):
        for o in (1, 2, 3):
            at = 1 + level * 3 + o - 1
            here = dst_of(o)
            remote(here, here, rsent.at[p, at], rrecv.at[p, at], peer["k"], False).wait_recv()

    def pos(p, level):
        return position(row, col, AXES[p][level])

    def cut(ref, p, j, size):
        return ref.at[p, pl.ds(pl.multiple_of(j * size, size), size), :]

    first, second = nb // 4, nb // 16

    def pair():
        for p in range(len(AXES)):
            remote(twin.at[p], twin.at[p], rsent.at[p, 0], rrecv.at[p, 0], peer["k"],
                   False).wait_recv()
            keep = pl.ds(pl.multiple_of(core * nb, nb), nb)
            paired[p] = mine[p, keep, :] + twin[p]
            exchange(p, 0, lambda j: cut(paired, p, j, first), lambda o: near.at[p, o - 1])

    def level_one():
        for p in range(len(AXES)):
            exchanged(p, 0, lambda o: near.at[p, o - 1])
            keep = pl.ds(pl.multiple_of(pos(p, 0) * first, first), first)
            nearest[p] = (paired[p, keep, :] + near[p, 0]) + (near[p, 1] + near[p, 2])
            exchange(p, 1, lambda j: cut(nearest, p, j, second), lambda o: mid.at[p, o - 1])

    def level_two():
        for p in range(len(AXES)):
            exchanged(p, 1, lambda o: mid.at[p, o - 1])
            keep = pl.ds(pl.multiple_of(pos(p, 1) * second, second), second)
            value = (nearest[p, keep, :] + mid[p, 0]) + (mid[p, 1] + mid[p, 2])
            middle[p] = value
            far[p, pos(p, 2)] = value
            here = pos(p, 2)
            exchange(p, 2, lambda j: middle.at[p], lambda o: far.at[p, here])

    def level_three():
        for p in range(len(AXES)):
            here = pos(p, 2)
            exchanged(p, 2, lambda o: far.at[p, (here + 4 - o) % 4])
            at = core * nb + pos(p, 0) * first + pos(p, 1) * second
            strip = pl.ds(pl.multiple_of(at, second), second)
            total[p, strip, :] = (far[p, 0] + far[p, 1]) + (far[p, 2] + far[p, 3])
            own = total.at[p, strip, :]
            exchange(p, 3, lambda j: own, lambda o: own)

    def strip_of(p, level, o):
        one = (pos(p, 0) + (4 - o if level == 4 else 0)) % 4
        if level == 4:
            return total.at[
                p, pl.ds(pl.multiple_of(core * nb + one * first, first), first), :]
        two = (pos(p, 1) + 4 - o) % 4
        at = core * nb + one * first + two * second
        return total.at[p, pl.ds(pl.multiple_of(at, second), second), :]

    def gather_one():
        for p in range(len(AXES)):
            exchanged(p, 3, lambda o: strip_of(p, 3, o))
            own = strip_of(p, 4, 0)
            exchange(p, 4, lambda j: own, lambda o: own)

    def gather_two():
        for p in range(len(AXES)):
            exchanged(p, 4, lambda o: strip_of(p, 4, o))
            own = cut(total, p, core, nb)
            remote(own, own, rsent.at[p, 16], rrecv.at[p, 16], peer["k"])

    def turn():
        for p in range(len(AXES)):
            here = cut(total, p, 1 - core, nb)
            remote(here, here, rsent.at[p, 16], rrecv.at[p, 16], peer["k"], False).wait_recv()
        last = len(AXES) - 1
        cross = jnp.concatenate(
            [total[last, :nb, wide - 128 :], total[last, nb:, wide - 128 :]], axis=1)
        keep = lax.broadcasted_iota(jnp.int32, (nb, nb), 0) <= lax.broadcasted_iota(
            jnp.int32, (nb, nb), 1)
        one = jnp.where(keep, factor_ref[0], 0.0)
        two = jnp.where(keep, factor_ref[1], 0.0)
        for p in range(len(AXES)):
            count = min(per, groups - p * per)
            at = pl.ds(p * wide, count * 128)
            s0 = total[p, :nb, : count * 128]
            c0 = dot3(one, s0)
            s1 = total[p, nb:, : count * 128] - dot3(cross, c0)
            c1 = dot3(two, s1)
            proj[:nb, at] = s0
            proj[nb:, at] = s1
            value = jnp.concatenate([tall[p * per + i] for i in range(count)], axis=1)
            value = value - (dot3(panel_ref[0], c0) + dot3(panel_ref[1], c1))
            high, low = split(value)
            parts[:rows, at] = high
            parts[rows:, at] = low


    own = pltpu.make_async_copy(m_ref, slot(HOME), local.at[0])

    def compute(g, begin, count):
        b, dy = g
        _, c = source(row, col, (0, b, dy, 0))
        q = [name for name, _ in order].index(g)
        if begin == 0:
            for d in OFFSETS:
                if group(d) == g:
                    shared(d)
            if g == group(HOME):
                own.wait()

        def unit(n, carry):
            at = pl.ds(pl.multiple_of(n * tile, tile), tile)
            m = full[c, :, at]
            high, low = split(m)
            both = jnp.dot(parts[...], high, preferred_element_type=F32)
            rest = jnp.dot(parts[:rows, :], low, preferred_element_type=F32)
            out_ref[:, pl.ds(pl.multiple_of(c * full.shape[2] + n * tile, tile), tile)] = both[:rows] + (both[rows:] + rest)
            line[...] += (m[:, :128] + m[:, 128:256]) + (m[:, 256:384] + m[:, 384:])
            return carry

        lax.fori_loop(begin, begin + count, unit, 0)

    def some(count):
        while count and todo:
            g, begin = todo.pop(0)
            take = min(count, tiles - begin)
            compute(g, begin, take)
            count -= take
            if begin + take < tiles:
                todo.insert(0, (g, begin + take))

    own.start()
    own_tall.start()
    line[...] = jnp.zeros_like(line)
    begin()
    pl.semaphore_wait(barrier, len(greeted))
    spread()
    steps = [landed, partial, pair, level_one, level_two, level_three, gather_one, gather_two, turn]
    tick = 0
    for t, plan in enumerate(PLAN):
        for half in range(HALVES):
            if tick == TICKS[0]:
                landed()
            for step, d, n in plan:
                arrive(d, half)
                send(step, d, n, half)
            if t == 0 and half == 0:
                share(HOME)
            for at, action in zip(TICKS, steps):
                if at == tick and action is not landed:
                    action()
            if tick >= TICKS[-1]:
                some(BATCH)
            tick += 1
        if t:
            for _, _, n in PLAN[t - 1]:
                for half in range(HALVES):
                    arrive(n, half)
                share(n)
        todo.extend((g, 0) for g, last in order if last == t - 1)
    some(len(order) * tiles)
    for _, _, n in PLAN[-1]:
        for half in range(HALVES):
            arrive(n, half)
        share(n)
    todo.extend((g, 0) for g, last in order if last == len(PLAN) - 1)
    some(len(order) * tiles)
    lanes = jnp.transpose(dot(proj[...], line[...]))
    sums = jnp.sum(lanes, axis=0, keepdims=True) / jnp.sqrt(F32(groups * full.shape[2]))
    wsum_ref[0:1, :] = sums[:, :nb]
    wsum_ref[1:2, :] = sums[:, nb:]
    for copy in started:
        copy.wait_send()


def per_device(basis, merge_coef, panels, factors):
    depth, span = merge_coef.shape
    groups = lax.axis_size("col")
    rows = basis.shape[0] // groups
    inner = basis.shape[1] * groups
    cols = span * groups
    nb = panels.shape[2]
    wide = (groups // len(AXES) + 1) * 128
    sems = pltpu.SemaphoreType.DMA
    vmem = lambda *shape: pltpu.VMEM(shape, F32)
    n = len(AXES)
    return pl.pallas_call(
        kernel,
        out_shape=(
            pltpu.VMEM((rows, cols), F32),
            pltpu.VMEM((2, nb), F32),
        ),
        in_specs=[pl.BlockSpec(memory_space=pltpu.VMEM)] * 4,
        out_specs=(pl.BlockSpec(memory_space=pltpu.VMEM), pl.BlockSpec(memory_space=pltpu.VMEM)),
        scratch_shapes=[
            vmem(groups, inner, span),
            pltpu.VMEM((2 * rows, inner), BF16),
            vmem(inner, 128),
            vmem(2 * nb, rows),
            vmem(groups, rows, 128),
            vmem(n, 2 * nb, wide),
            vmem(n, nb, wide),
            vmem(n, nb, wide),
            vmem(n, 3, nb // 4, wide),
            vmem(n, nb // 4, wide),
            vmem(n, 3, nb // 16, wide),
            vmem(n, nb // 16, wide),
            vmem(n, 4, nb // 16, wide),
            vmem(n, 2 * nb, wide),
            vmem(2 * nb, inner),
            sems((len(OFFSETS), HALVES)),
            sems((len(OFFSETS), HALVES)),
            sems((len(OFFSETS),)),
            sems((len(OFFSETS),)),
            sems((2,)),
            sems((groups,)),
            sems((groups - 1,)),
            sems((groups - 1,)),
            sems((n, 17)),
            sems((n, 17)),
        ],
        compiler_params=pltpu.CompilerParams(
            collective_id=0, has_side_effects=True, vmem_limit_bytes=54 * 2**20
        ),
        cost_estimate=pl.CostEstimate(
            flops=6 * rows * inner * cols, bytes_accessed=4 * rows * cols, transcendentals=0
        ),
    )(merge_coef, basis, panels, factors)


def solution(mesh):
    return jax.shard_map(
        per_device,
        mesh=mesh,
        in_specs=(P("row", "col"), P("row", "col"), P(None, ("row", "col"), None), P()),
        out_specs=(P(("row", "col"), None), P()),
        check_vma=False,
    )
```

```python
import functools

import jax
import jax.numpy as jnp
from jax import lax
from jax.experimental import pallas as pl
from jax.experimental.pallas import tpu as pltpu
from jax.sharding import PartitionSpec as P

HI = lax.Precision.HIGHEST
MESH = pl.DeviceIdType.MESH
F32 = jnp.float32
BF16 = jnp.bfloat16

STEPS = ("a", "b", "y+", "y-", "z+", "z-")
OFFSETS = tuple((a, b, y, z) for a in (0, 1) for b in (0, 1) for y in range(4) for z in range(4))
INDEX = {d: i for i, d in enumerate(OFFSETS)}
HOME = (0, 0, 0, 0)
ROUNDS = (
    ((3, 0), (5, 0), (2, 0), (4, 0), (0, 0), (1, 0)),
    ((5, 32), (4, 32), (3, 3), (0, 16), (1, 1), (2, 32)),
    ((0, 17), (1, 35), (5, 3), (4, 33), (2, 35), (3, 35)),
    ((0, 51), (4, 49), (5, 4), (1, 2), (2, 34), (3, 1)),
    ((0, 38), (5, 38), (4, 4), (1, 4), (3, 2), (2, 36)),
    ((4, 47), (5, 47), (0, 13), (1, 5), (3, 15), (2, 37)),
    ((5, 40), (4, 11), (0, 41), (2, 6), (3, 46), (1, 36)),
    ((0, 21), (4, 21), (5, 52), (3, 19), (2, 50), (1, 7)),
    ((0, 31), (5, 31), (4, 31), (3, 48), (2, 52), (1, 13)),
    ((5, 63), (4, 60), (0, 56), (3, 63), (2, 21), (1, 10)),
    ((4, 26), (5, 59), (3, 61)),
)
HALVES = 4


def onward(d, step):
    a, b, y, z = d
    if step == "a":
        return 1 - a, b, y, z
    if step == "b":
        return a, 1 - b, y, z
    if step in ("y+", "y-"):
        return a, b, (y + (1 if step == "y+" else 3)) % 4, z
    return a, b, y, (z + (1 if step == "z+" else 3)) % 4


PLAN = tuple(
    tuple((STEPS[s], OFFSETS[i], onward(OFFSETS[i], STEPS[s])) for s, i in line) for line in ROUNDS
)


def coords(row, col):
    return row // 8, (row // 2) % 4, row % 2, col // 4, col % 4


def place(xl, z, k, xh, y):
    return xl * 8 + z * 2 + k, xh * 4 + y


def neighbour(row, col, step):
    xl, z, k, xh, y = coords(row, col)
    if step == "a":
        xl = 1 - xl
    elif step == "b":
        xl, xh = 1 - xl, 1 - xh
    elif step == "y+":
        y = (y + 1) % 4
    elif step == "y-":
        y = (y + 3) % 4
    elif step == "z+":
        z = (z + 1) % 4
    elif step == "z-":
        z = (z + 3) % 4
    else:
        k = 1 - k
    return place(xl, z, k, xh, y)


def source(row, col, d, other=0):
    xl, z, k, xh, y = coords(row, col)
    a, b, dy, dz = d
    return place(
        (xl + a + b) % 2, (z + 4 - dz) % 4, (k + other) % 2, (xh + b) % 2, (y + 4 - dy) % 4
    )


def group(d):
    return d[1], d[2]


def group_order():
    last = {}
    for t, line in enumerate(PLAN):
        for _, _, n in line:
            last[group(n)] = t
    return sorted(last.items(), key=lambda kv: kv[1])


def split(x):
    high = x.astype(BF16)
    return high, (x - high.astype(F32)).astype(BF16)


def dot(left, right, precision=HI):
    return jnp.dot(left, right, precision=precision, preferred_element_type=F32)


def dot3(left, right):
    (a, b), (c, d) = split(left), split(right)
    part = functools.partial(jnp.dot, preferred_element_type=F32)
    return part(a, c) + (part(a, d) + part(b, c))


AXES = (("z", "y", "x"), ("y", "x", "z"), ("x", "z", "y"))
TICKS = (8, 8, 10, 14, 17, 20, 23, 26, 30)
TURNS = (2, 0, 1)
STAGGER = 1
BATCH = 1


def along(row, col, axis, step):
    xl, z, k, xh, y = coords(row, col)
    if axis == "x":
        x = (xh * 2 + xl + step) % 4
        xl, xh = x % 2, x // 2
    elif axis == "y":
        y = (y + step) % 4
    else:
        z = (z + step) % 4
    return place(xl, z, k, xh, y)


def position(row, col, axis):
    xl, z, _, xh, y = coords(row, col)
    return {"x": xh * 2 + xl, "y": y, "z": z}[axis]


def kernel(
    m_ref, basis_ref, panel_ref, factor_ref, out_ref, wsum_ref,
    full, parts, line, turned, tall, mine, twin, paired, near, nearest, mid, middle, far, total, proj,
    recv, sent, krecv, ksent, local, outsem, trecv, tsent, rrecv, rsent,
):
    row = lax.axis_index("row")
    col = lax.axis_index("col")
    _, _, core, _, _ = coords(row, col)
    depth = m_ref.shape[0]
    piece = depth // HALVES
    tile = 512
    tiles = full.shape[2] // tile
    groups = full.shape[0]
    rows = out_ref.shape[0]
    nb = panel_ref.shape[2]
    peer = {step: neighbour(row, col, step) for step in STEPS + ("k",)}

    barrier = pltpu.get_barrier_semaphore()
    greeted = [(row, (col + o) % groups) for o in range(1, groups)]
    greeted += [along(row, col, "x", o) for o in (1, 3)]
    greeted += [along(row, col, "z", o) for o in (1, 2, 3)]
    greeted += [peer["k"]]
    for device in greeted:
        pl.semaphore_signal(barrier, inc=1, device_id=device, device_id_type=MESH)
    started = []
    stores = []
    arrived = set()
    todo = []
    order = group_order()

    def remote(src, dst, out_sem, in_sem, device, start=True):
        copy = pltpu.make_async_remote_copy(
            src, dst, out_sem, in_sem, device, device_id_type=MESH)
        if start:
            copy.start()
            started.append(copy)
        return copy


    def slot(d, other=0, half=None):
        r, c = source(row, col, d, other)
        if half is None:
            return full.at[c, pl.ds(pl.multiple_of(r * depth, depth), depth), :]
        return full.at[c, pl.ds(pl.multiple_of(r * depth + half * piece, piece), piece), :]

    def held(d, half=None):
        if d == HOME:
            return m_ref if half is None else m_ref.at[pl.ds(half * piece, piece), :]
        return slot(d, 0, half)

    def send(step, d, n, half):
        i = INDEX[n]
        remote(held(d, half), slot(d, 0, half), sent.at[i, half], recv.at[i, half], peer[step])

    def arrive(n, half):
        if (n, half) in arrived or n == HOME:
            return
        arrived.add((n, half))
        i, here = INDEX[n], slot(n, 0, half)
        remote(here, here, sent.at[i, half], recv.at[i, half], peer["k"], False).wait_recv()

    def share(d):
        remote(held(d), slot(d), ksent.at[INDEX[d]], krecv.at[INDEX[d]], peer["k"])

    def shared(d):
        i, here = INDEX[d], slot(d, 1)
        remote(here, here, ksent.at[i], krecv.at[i], peer["k"], False).wait_recv()


    def block(j):
        return basis_ref.at[pl.ds(pl.multiple_of(j * rows, rows), rows), :]

    own_tall = pltpu.make_async_copy(block(col), tall.at[col], local.at[1])

    def spread():
        for o in range(1, groups):
            j = (col + o) % groups
            remote(block(j), tall.at[col], tsent.at[o - 1], trecv.at[o - 1], (row, j))


    wide = total.shape[2]
    per = wide // 128

    def begin():
        value = jnp.transpose(jnp.concatenate([panel_ref[0], panel_ref[1]], axis=1))
        turned[...] = value
        cross = dot3(value[nb:], panel_ref[0])
        last = len(AXES) - 1
        mine[last, :nb, wide - 128 :] = cross[:, :128]
        mine[last, nb:, wide - 128 :] = cross[:, 128:]

    def landed():
        own_tall.wait()
        for o in range(1, groups):
            here = tall.at[(col + groups - o) % groups]
            remote(here, here, tsent.at[o - 1], trecv.at[o - 1], peer["k"], False).wait_recv()

    def partial(parts_now):
        for p in parts_now:
            count = min(per, groups - p * per)
            value = jnp.concatenate([tall[p * per + i] for i in range(count)], axis=1)
            mine[p, :, : count * 128] = dot3(turned[...], value)
            other = pl.ds(pl.multiple_of((1 - core) * nb, nb), nb)
            remote(mine.at[p, other], twin.at[p], rsent.at[p, 0], rrecv.at[p, 0], peer["k"])

    def exchange(p, level, src_of, dst_of):
        axis = AXES[p][(0, 1, 2, 1, 0)[level]]
        for o in (1, 2, 3):
            j = (position(row, col, axis) + o) % 4
            at = 1 + level * 3 + o - 1
            remote(src_of(j), dst_of(o), rsent.at[p, at], rrecv.at[p, at],
                   along(row, col, axis, o))

    def exchanged(p, level, dst_of):
        for o in (1, 2, 3):
            at = 1 + level * 3 + o - 1
            here = dst_of(o)
            remote(here, here, rsent.at[p, at], rrecv.at[p, at], peer["k"], False).wait_recv()

    def pos(p, level):
        return position(row, col, AXES[p][level])

    def cut(ref, p, j, size):
        return ref.at[p, pl.ds(pl.multiple_of(j * size, size), size), :]

    first, second = nb // 4, nb // 16

    def pair(parts_now):
        for p in parts_now:
            remote(twin.at[p], twin.at[p], rsent.at[p, 0], rrecv.at[p, 0], peer["k"],
                   False).wait_recv()
            keep = pl.ds(pl.multiple_of(core * nb, nb), nb)
            paired[p] = mine[p, keep, :] + twin[p]
            exchange(p, 0, lambda j: cut(paired, p, j, first), lambda o: near.at[p, o - 1])

    def level_one(parts_now):
        for p in parts_now:
            exchanged(p, 0, lambda o: near.at[p, o - 1])
            keep = pl.ds(pl.multiple_of(pos(p, 0) * first, first), first)
            nearest[p] = (paired[p, keep, :] + near[p, 0]) + (near[p, 1] + near[p, 2])
            exchange(p, 1, lambda j: cut(nearest, p, j, second), lambda o: mid.at[p, o - 1])

    def level_two(parts_now):
        for p in parts_now:
            exchanged(p, 1, lambda o: mid.at[p, o - 1])
            keep = pl.ds(pl.multiple_of(pos(p, 1) * second, second), second)
            value = (nearest[p, keep, :] + mid[p, 0]) + (mid[p, 1] + mid[p, 2])
            middle[p] = value
            far[p, pos(p, 2)] = value
            here = pos(p, 2)
            exchange(p, 2, lambda j: middle.at[p], lambda o: far.at[p, here])

    def level_three(parts_now):
        for p in parts_now:
            here = pos(p, 2)
            exchanged(p, 2, lambda o: far.at[p, (here + 4 - o) % 4])
            at = core * nb + pos(p, 0) * first + pos(p, 1) * second
            strip = pl.ds(pl.multiple_of(at, second), second)
            total[p, strip, :] = (far[p, 0] + far[p, 1]) + (far[p, 2] + far[p, 3])
            own = total.at[p, strip, :]
            exchange(p, 3, lambda j: own, lambda o: own)

    def strip_of(p, level, o):
        one = (pos(p, 0) + (4 - o if level == 4 else 0)) % 4
        if level == 4:
            return total.at[
                p, pl.ds(pl.multiple_of(core * nb + one * first, first), first), :]
        two = (pos(p, 1) + 4 - o) % 4
        at = core * nb + one * first + two * second
        return total.at[p, pl.ds(pl.multiple_of(at, second), second), :]

    def gather_one(parts_now):
        for p in parts_now:
            exchanged(p, 3, lambda o: strip_of(p, 3, o))
            own = strip_of(p, 4, 0)
            exchange(p, 4, lambda j: own, lambda o: own)

    def gather_two(parts_now):
        for p in parts_now:
            exchanged(p, 4, lambda o: strip_of(p, 4, o))
            own = cut(total, p, core, nb)
            remote(own, own, rsent.at[p, 16], rrecv.at[p, 16], peer["k"])

    def turn(parts_now):
        for p in parts_now:
            here = cut(total, p, 1 - core, nb)
            remote(here, here, rsent.at[p, 16], rrecv.at[p, 16], peer["k"], False).wait_recv()
        last = len(AXES) - 1
        cross = jnp.concatenate(
            [total[last, :nb, wide - 128 :], total[last, nb:, wide - 128 :]], axis=1)
        keep = lax.broadcasted_iota(jnp.int32, (nb, nb), 0) <= lax.broadcasted_iota(
            jnp.int32, (nb, nb), 1)
        one = jnp.where(keep, factor_ref[0], 0.0)
        two = jnp.where(keep, factor_ref[1], 0.0)
        for p in parts_now:
            count = min(per, groups - p * per)
            at = pl.ds(p * wide, count * 128)
            s0 = total[p, :nb, : count * 128]
            c0 = dot3(one, s0)
            s1 = total[p, nb:, : count * 128] - dot3(cross, c0)
            c1 = dot3(two, s1)
            proj[:nb, at] = s0
            proj[nb:, at] = s1
            value = jnp.concatenate([tall[p * per + i] for i in range(count)], axis=1)
            value = value - (dot3(panel_ref[0], c0) + dot3(panel_ref[1], c1))
            high, low = split(value)
            parts[:rows, at] = high
            parts[rows:, at] = low


    own = pltpu.make_async_copy(m_ref, slot(HOME), local.at[0])

    def compute(g, begin, count):
        b, dy = g
        _, c = source(row, col, (0, b, dy, 0))
        q = [name for name, _ in order].index(g)
        if begin == 0:
            for d in OFFSETS:
                if group(d) == g:
                    shared(d)
            if g == group(HOME):
                own.wait()

        def unit(n, carry):
            at = pl.ds(pl.multiple_of(n * tile, tile), tile)
            m = full[c, :, at]
            high, low = split(m)
            both = jnp.dot(parts[...], high, preferred_element_type=F32)
            rest = jnp.dot(parts[:rows, :], low, preferred_element_type=F32)
            out_ref[:, pl.ds(pl.multiple_of(c * full.shape[2] + n * tile, tile), tile)] = both[:rows] + (both[rows:] + rest)
            line[...] += (m[:, :128] + m[:, 128:256]) + (m[:, 256:384] + m[:, 384:])
            return carry

        lax.fori_loop(begin, begin + count, unit, 0)

    def some(count):
        while count and todo:
            g, begin = todo.pop(0)
            take = min(count, tiles - begin)
            compute(g, begin, take)
            count -= take
            if begin + take < tiles:
                todo.insert(0, (g, begin + take))

    own.start()
    own_tall.start()
    line[...] = jnp.zeros_like(line)
    begin()
    pl.semaphore_wait(barrier, len(greeted))
    spread()
    steps = [partial, pair, level_one, level_two, level_three, gather_one, gather_two, turn]
    tick = 0
    for t, plan in enumerate(PLAN):
        for half in range(HALVES):
            if tick == TICKS[0]:
                landed()
            for step, d, n in plan:
                arrive(d, half)
                send(step, d, n, half)
            if t == 0 and half == 0:
                share(HOME)
            for at, action in zip(TICKS[1:], steps):
                for i, p in enumerate(TURNS):
                    if at + i * STAGGER == tick:
                        action((p,))
            if tick >= TICKS[-1] + (len(TURNS) - 1) * STAGGER:
                some(BATCH)
            tick += 1
        if t:
            for _, _, n in PLAN[t - 1]:
                for half in range(HALVES):
                    arrive(n, half)
                share(n)
        todo.extend((g, 0) for g, last in order if last == t - 1)
    some(len(order) * tiles)
    for _, _, n in PLAN[-1]:
        for half in range(HALVES):
            arrive(n, half)
        share(n)
    todo.extend((g, 0) for g, last in order if last == len(PLAN) - 1)
    some(len(order) * tiles)
    lanes = jnp.transpose(dot(proj[...], line[...]))
    sums = jnp.sum(lanes, axis=0, keepdims=True) / jnp.sqrt(F32(groups * full.shape[2]))
    wsum_ref[0:1, :] = sums[:, :nb]
    wsum_ref[1:2, :] = sums[:, nb:]
    for copy in started:
        copy.wait_send()


def per_device(basis, merge_coef, panels, factors):
    depth, span = merge_coef.shape
    groups = lax.axis_size("col")
    rows = basis.shape[0] // groups
    inner = basis.shape[1] * groups
    cols = span * groups
    nb = panels.shape[2]
    wide = (groups // len(AXES) + 1) * 128
    sems = pltpu.SemaphoreType.DMA
    vmem = lambda *shape: pltpu.VMEM(shape, F32)
    n = len(AXES)
    return pl.pallas_call(
        kernel,
        out_shape=(
            pltpu.VMEM((rows, cols), F32),
            pltpu.VMEM((2, nb), F32),
        ),
        in_specs=[pl.BlockSpec(memory_space=pltpu.VMEM)] * 4,
        out_specs=(pl.BlockSpec(memory_space=pltpu.VMEM), pl.BlockSpec(memory_space=pltpu.VMEM)),
        scratch_shapes=[
            vmem(groups, inner, span),
            pltpu.VMEM((2 * rows, inner), BF16),
            vmem(inner, 128),
            vmem(2 * nb, rows),
            vmem(groups, rows, 128),
            vmem(n, 2 * nb, wide),
            vmem(n, nb, wide),
            vmem(n, nb, wide),
            vmem(n, 3, nb // 4, wide),
            vmem(n, nb // 4, wide),
            vmem(n, 3, nb // 16, wide),
            vmem(n, nb // 16, wide),
            vmem(n, 4, nb // 16, wide),
            vmem(n, 2 * nb, wide),
            vmem(2 * nb, inner),
            sems((len(OFFSETS), HALVES)),
            sems((len(OFFSETS), HALVES)),
            sems((len(OFFSETS),)),
            sems((len(OFFSETS),)),
            sems((2,)),
            sems((groups,)),
            sems((groups - 1,)),
            sems((groups - 1,)),
            sems((n, 17)),
            sems((n, 17)),
        ],
        compiler_params=pltpu.CompilerParams(
            collective_id=0, has_side_effects=True, vmem_limit_bytes=54 * 2**20
        ),
        cost_estimate=pl.CostEstimate(
            flops=6 * rows * inner * cols, bytes_accessed=4 * rows * cols, transcendentals=0
        ),
    )(merge_coef, basis, panels, factors)


def solution(mesh):
    return jax.shard_map(
        per_device,
        mesh=mesh,
        in_specs=(P("row", "col"), P("row", "col"), P(None, ("row", "col"), None), P()),
        out_specs=(P(("row", "col"), None), P()),
        check_vma=False,
    )
```

```python
import functools

import jax
import jax.numpy as jnp
from jax import lax
from jax.experimental import pallas as pl
from jax.experimental.pallas import tpu as pltpu
from jax.sharding import PartitionSpec as P

HI = lax.Precision.HIGHEST
MESH = pl.DeviceIdType.MESH
F32 = jnp.float32
BF16 = jnp.bfloat16

STEPS = ("a", "b", "y+", "y-", "z+", "z-")
OFFSETS = tuple((a, b, y, z) for a in (0, 1) for b in (0, 1) for y in range(4) for z in range(4))
INDEX = {d: i for i, d in enumerate(OFFSETS)}
HOME = (0, 0, 0, 0)
ROUNDS = (
    ((3, 0), (5, 0), (2, 0), (4, 0), (0, 0), (1, 0)),
    ((5, 32), (4, 32), (3, 3), (0, 16), (1, 1), (2, 32)),
    ((0, 17), (1, 35), (5, 3), (4, 33), (2, 35), (3, 35)),
    ((0, 51), (4, 49), (5, 4), (1, 2), (2, 34), (3, 1)),
    ((0, 38), (5, 38), (4, 4), (1, 4), (3, 2), (2, 36)),
    ((4, 47), (5, 47), (0, 13), (1, 5), (3, 15), (2, 37)),
    ((5, 40), (4, 11), (0, 41), (2, 6), (3, 46), (1, 36)),
    ((0, 21), (4, 21), (5, 52), (3, 19), (2, 50), (1, 7)),
    ((0, 31), (5, 31), (4, 31), (3, 48), (2, 52), (1, 13)),
    ((5, 63), (4, 60), (0, 56), (3, 63), (2, 21), (1, 10)),
    ((4, 26), (5, 59), (3, 61)),
)
HALVES = 4


def onward(d, step):
    a, b, y, z = d
    if step == "a":
        return 1 - a, b, y, z
    if step == "b":
        return a, 1 - b, y, z
    if step in ("y+", "y-"):
        return a, b, (y + (1 if step == "y+" else 3)) % 4, z
    return a, b, y, (z + (1 if step == "z+" else 3)) % 4


PLAN = tuple(
    tuple((STEPS[s], OFFSETS[i], onward(OFFSETS[i], STEPS[s])) for s, i in line) for line in ROUNDS
)


def coords(row, col):
    return row // 8, (row // 2) % 4, row % 2, col // 4, col % 4


def place(xl, z, k, xh, y):
    return xl * 8 + z * 2 + k, xh * 4 + y


def neighbour(row, col, step):
    xl, z, k, xh, y = coords(row, col)
    if step == "a":
        xl = 1 - xl
    elif step == "b":
        xl, xh = 1 - xl, 1 - xh
    elif step == "y+":
        y = (y + 1) % 4
    elif step == "y-":
        y = (y + 3) % 4
    elif step == "z+":
        z = (z + 1) % 4
    elif step == "z-":
        z = (z + 3) % 4
    else:
        k = 1 - k
    return place(xl, z, k, xh, y)


def source(row, col, d, other=0):
    xl, z, k, xh, y = coords(row, col)
    a, b, dy, dz = d
    return place(
        (xl + a + b) % 2, (z + 4 - dz) % 4, (k + other) % 2, (xh + b) % 2, (y + 4 - dy) % 4
    )


def group(d):
    return d[1], d[2]


def group_order():
    last = {}
    for t, line in enumerate(PLAN):
        for _, _, n in line:
            last[group(n)] = t
    return sorted(last.items(), key=lambda kv: kv[1])


def split(x):
    high = x.astype(BF16)
    return high, (x - high.astype(F32)).astype(BF16)


def dot(left, right, precision=HI):
    return jnp.dot(left, right, precision=precision, preferred_element_type=F32)


def dot3(left, right):
    (a, b), (c, d) = split(left), split(right)
    part = functools.partial(jnp.dot, preferred_element_type=F32)
    return part(a, c) + (part(a, d) + part(b, c))


AXES = (("z", "y", "x"), ("y", "x", "z"), ("x", "z", "y"))
TICKS = (8, 8, 10, 14, 17, 20, 23, 26, 30)
TURNS = (2, 0, 1)
STAGGER = 1
BATCH = 1


def along(row, col, axis, step):
    xl, z, k, xh, y = coords(row, col)
    if axis == "x":
        x = (xh * 2 + xl + step) % 4
        xl, xh = x % 2, x // 2
    elif axis == "y":
        y = (y + step) % 4
    else:
        z = (z + step) % 4
    return place(xl, z, k, xh, y)


def position(row, col, axis):
    xl, z, _, xh, y = coords(row, col)
    return {"x": xh * 2 + xl, "y": y, "z": z}[axis]


def kernel(
    m_ref, basis_ref, panel_ref, factor_ref, out_ref, wsum_ref,
    full, parts, line, turned, tall, mine, twin, paired, near, nearest, mid, middle, far, total, proj,
    recv, sent, krecv, ksent, local, outsem, trecv, tsent, rrecv, rsent,
):
    row = lax.axis_index("row")
    col = lax.axis_index("col")
    _, _, core, _, _ = coords(row, col)
    depth = m_ref.shape[0]
    piece = depth // HALVES
    tile = 512
    tiles = full.shape[2] // tile
    groups = full.shape[0]
    rows = out_ref.shape[0]
    nb = panel_ref.shape[2]
    peer = {step: neighbour(row, col, step) for step in STEPS + ("k",)}

    barrier = pltpu.get_barrier_semaphore()
    greeted = [(row, (col + o) % groups) for o in range(1, groups)]
    greeted += [along(row, col, "x", o) for o in (1, 3)]
    greeted += [along(row, col, "z", o) for o in (1, 2, 3)]
    greeted += [peer["k"]]
    for device in greeted:
        pl.semaphore_signal(barrier, inc=1, device_id=device, device_id_type=MESH)
    started = []
    stores = []
    arrived = set()
    todo = []
    order = group_order()

    def remote(src, dst, out_sem, in_sem, device, start=True):
        copy = pltpu.make_async_remote_copy(
            src, dst, out_sem, in_sem, device, device_id_type=MESH)
        if start:
            copy.start()
            started.append(copy)
        return copy


    def slot(d, other=0, half=None):
        r, c = source(row, col, d, other)
        if half is None:
            return full.at[c, pl.ds(pl.multiple_of(r * depth, depth), depth), :]
        return full.at[c, pl.ds(pl.multiple_of(r * depth + half * piece, piece), piece), :]

    def held(d, half=None):
        if d == HOME:
            return m_ref if half is None else m_ref.at[pl.ds(half * piece, piece), :]
        return slot(d, 0, half)

    def send(step, d, n, half):
        i = INDEX[n]
        remote(held(d, half), slot(d, 0, half), sent.at[i, half], recv.at[i, half], peer[step])

    def arrive(n, half):
        if (n, half) in arrived or n == HOME:
            return
        arrived.add((n, half))
        i, here = INDEX[n], slot(n, 0, half)
        remote(here, here, sent.at[i, half], recv.at[i, half], peer["k"], False).wait_recv()

    final = {n for _, _, n in PLAN[-1]}

    def share(d, half=None):
        i, at = INDEX[d], half or 0
        remote(held(d, half), slot(d, 0, half), ksent.at[i, at], krecv.at[i, at], peer["k"])

    def shared(d):
        for half in range(HALVES) if d in final else (None,):
            i, at, here = INDEX[d], half or 0, slot(d, 1, half)
            remote(here, here, ksent.at[i, at], krecv.at[i, at], peer["k"], False).wait_recv()


    def block(j):
        return basis_ref.at[pl.ds(pl.multiple_of(j * rows, rows), rows), :]

    own_tall = pltpu.make_async_copy(block(col), tall.at[col], local.at[1])

    def spread():
        for o in range(1, groups):
            j = (col + o) % groups
            remote(block(j), tall.at[col], tsent.at[o - 1], trecv.at[o - 1], (row, j))


    wide = total.shape[2]
    per = wide // 128

    def begin():
        value = jnp.transpose(jnp.concatenate([panel_ref[0], panel_ref[1]], axis=1))
        turned[...] = value
        cross = dot3(value[nb:], panel_ref[0])
        last = len(AXES) - 1
        mine[last, :nb, wide - 128 :] = cross[:, :128]
        mine[last, nb:, wide - 128 :] = cross[:, 128:]

    def landed():
        own_tall.wait()
        for o in range(1, groups):
            here = tall.at[(col + groups - o) % groups]
            remote(here, here, tsent.at[o - 1], trecv.at[o - 1], peer["k"], False).wait_recv()

    def partial(parts_now):
        for p in parts_now:
            count = min(per, groups - p * per)
            value = jnp.concatenate([tall[p * per + i] for i in range(count)], axis=1)
            mine[p, :, : count * 128] = dot3(turned[...], value)
            other = pl.ds(pl.multiple_of((1 - core) * nb, nb), nb)
            remote(mine.at[p, other], twin.at[p], rsent.at[p, 0], rrecv.at[p, 0], peer["k"])

    def exchange(p, level, src_of, dst_of):
        axis = AXES[p][(0, 1, 2, 1, 0)[level]]
        for o in (1, 2, 3):
            j = (position(row, col, axis) + o) % 4
            at = 1 + level * 3 + o - 1
            remote(src_of(j), dst_of(o), rsent.at[p, at], rrecv.at[p, at],
                   along(row, col, axis, o))

    def exchanged(p, level, dst_of):
        for o in (1, 2, 3):
            at = 1 + level * 3 + o - 1
            here = dst_of(o)
            remote(here, here, rsent.at[p, at], rrecv.at[p, at], peer["k"], False).wait_recv()

    def pos(p, level):
        return position(row, col, AXES[p][level])

    def cut(ref, p, j, size):
        return ref.at[p, pl.ds(pl.multiple_of(j * size, size), size), :]

    first, second = nb // 4, nb // 16

    def pair(parts_now):
        for p in parts_now:
            remote(twin.at[p], twin.at[p], rsent.at[p, 0], rrecv.at[p, 0], peer["k"],
                   False).wait_recv()
            keep = pl.ds(pl.multiple_of(core * nb, nb), nb)
            paired[p] = mine[p, keep, :] + twin[p]
            exchange(p, 0, lambda j: cut(paired, p, j, first), lambda o: near.at[p, o - 1])

    def level_one(parts_now):
        for p in parts_now:
            exchanged(p, 0, lambda o: near.at[p, o - 1])
            keep = pl.ds(pl.multiple_of(pos(p, 0) * first, first), first)
            nearest[p] = (paired[p, keep, :] + near[p, 0]) + (near[p, 1] + near[p, 2])
            exchange(p, 1, lambda j: cut(nearest, p, j, second), lambda o: mid.at[p, o - 1])

    def level_two(parts_now):
        for p in parts_now:
            exchanged(p, 1, lambda o: mid.at[p, o - 1])
            keep = pl.ds(pl.multiple_of(pos(p, 1) * second, second), second)
            value = (nearest[p, keep, :] + mid[p, 0]) + (mid[p, 1] + mid[p, 2])
            middle[p] = value
            far[p, pos(p, 2)] = value
            here = pos(p, 2)
            exchange(p, 2, lambda j: middle.at[p], lambda o: far.at[p, here])

    def level_three(parts_now):
        for p in parts_now:
            here = pos(p, 2)
            exchanged(p, 2, lambda o: far.at[p, (here + 4 - o) % 4])
            at = core * nb + pos(p, 0) * first + pos(p, 1) * second
            strip = pl.ds(pl.multiple_of(at, second), second)
            total[p, strip, :] = (far[p, 0] + far[p, 1]) + (far[p, 2] + far[p, 3])
            own = total.at[p, strip, :]
            exchange(p, 3, lambda j: own, lambda o: own)

    def strip_of(p, level, o):
        one = (pos(p, 0) + (4 - o if level == 4 else 0)) % 4
        if level == 4:
            return total.at[
                p, pl.ds(pl.multiple_of(core * nb + one * first, first), first), :]
        two = (pos(p, 1) + 4 - o) % 4
        at = core * nb + one * first + two * second
        return total.at[p, pl.ds(pl.multiple_of(at, second), second), :]

    def gather_one(parts_now):
        for p in parts_now:
            exchanged(p, 3, lambda o: strip_of(p, 3, o))
            own = strip_of(p, 4, 0)
            exchange(p, 4, lambda j: own, lambda o: own)

    def gather_two(parts_now):
        for p in parts_now:
            exchanged(p, 4, lambda o: strip_of(p, 4, o))
            own = cut(total, p, core, nb)
            remote(own, own, rsent.at[p, 16], rrecv.at[p, 16], peer["k"])

    def turn(parts_now):
        for p in parts_now:
            here = cut(total, p, 1 - core, nb)
            remote(here, here, rsent.at[p, 16], rrecv.at[p, 16], peer["k"], False).wait_recv()
        last = len(AXES) - 1
        cross = jnp.concatenate(
            [total[last, :nb, wide - 128 :], total[last, nb:, wide - 128 :]], axis=1)
        keep = lax.broadcasted_iota(jnp.int32, (nb, nb), 0) <= lax.broadcasted_iota(
            jnp.int32, (nb, nb), 1)
        one = jnp.where(keep, factor_ref[0], 0.0)
        two = jnp.where(keep, factor_ref[1], 0.0)
        for p in parts_now:
            count = min(per, groups - p * per)
            at = pl.ds(p * wide, count * 128)
            s0 = total[p, :nb, : count * 128]
            c0 = dot3(one, s0)
            s1 = total[p, nb:, : count * 128] - dot3(cross, c0)
            c1 = dot3(two, s1)
            proj[:nb, at] = s0
            proj[nb:, at] = s1
            value = jnp.concatenate([tall[p * per + i] for i in range(count)], axis=1)
            value = value - (dot3(panel_ref[0], c0) + dot3(panel_ref[1], c1))
            high, low = split(value)
            parts[:rows, at] = high
            parts[rows:, at] = low


    own = pltpu.make_async_copy(m_ref, slot(HOME), local.at[0])

    def compute(g, begin, count):
        b, dy = g
        _, c = source(row, col, (0, b, dy, 0))
        q = [name for name, _ in order].index(g)
        if begin == 0:
            for d in OFFSETS:
                if group(d) == g:
                    shared(d)
            if g == group(HOME):
                own.wait()

        def unit(n, carry):
            at = pl.ds(pl.multiple_of(n * tile, tile), tile)
            m = full[c, :, at]
            high, low = split(m)
            both = jnp.dot(parts[...], high, preferred_element_type=F32)
            rest = jnp.dot(parts[:rows, :], low, preferred_element_type=F32)
            out_ref[:, pl.ds(pl.multiple_of(c * full.shape[2] + n * tile, tile), tile)] = both[:rows] + (both[rows:] + rest)
            line[...] += (m[:, :128] + m[:, 128:256]) + (m[:, 256:384] + m[:, 384:])
            return carry

        lax.fori_loop(begin, begin + count, unit, 0)

    def some(count):
        while count and todo:
            g, begin = todo.pop(0)
            take = min(count, tiles - begin)
            compute(g, begin, take)
            count -= take
            if begin + take < tiles:
                todo.insert(0, (g, begin + take))

    own.start()
    own_tall.start()
    line[...] = jnp.zeros_like(line)
    begin()
    pl.semaphore_wait(barrier, len(greeted))
    spread()
    steps = [partial, pair, level_one, level_two, level_three, gather_one, gather_two, turn]
    tick = 0
    for t, plan in enumerate(PLAN):
        for half in range(HALVES):
            if tick == TICKS[0]:
                landed()
            for step, d, n in plan:
                arrive(d, half)
                send(step, d, n, half)
            if t == 0 and half == 0:
                share(HOME)
            for at, action in zip(TICKS[1:], steps):
                for i, p in enumerate(TURNS):
                    if at + i * STAGGER == tick:
                        action((p,))
            if tick >= TICKS[-1] + (len(TURNS) - 1) * STAGGER:
                some(BATCH)
            tick += 1
        if t:
            for _, _, n in PLAN[t - 1]:
                for half in range(HALVES):
                    arrive(n, half)
                share(n)
        todo.extend((g, 0) for g, last in order if last == t - 1)
    some(len(order) * tiles)
    for half in range(HALVES):
        for _, _, n in PLAN[-1]:
            arrive(n, half)
            share(n, half)
    todo.extend((g, 0) for g, last in order if last == len(PLAN) - 1)
    some(len(order) * tiles)
    lanes = jnp.transpose(dot(proj[...], line[...]))
    sums = jnp.sum(lanes, axis=0, keepdims=True) / jnp.sqrt(F32(groups * full.shape[2]))
    wsum_ref[0:1, :] = sums[:, :nb]
    wsum_ref[1:2, :] = sums[:, nb:]
    for copy in started:
        copy.wait_send()


def per_device(basis, merge_coef, panels, factors):
    depth, span = merge_coef.shape
    groups = lax.axis_size("col")
    rows = basis.shape[0] // groups
    inner = basis.shape[1] * groups
    cols = span * groups
    nb = panels.shape[2]
    wide = (groups // len(AXES) + 1) * 128
    sems = pltpu.SemaphoreType.DMA
    vmem = lambda *shape: pltpu.VMEM(shape, F32)
    n = len(AXES)
    return pl.pallas_call(
        kernel,
        out_shape=(
            pltpu.VMEM((rows, cols), F32),
            pltpu.VMEM((2, nb), F32),
        ),
        in_specs=[pl.BlockSpec(memory_space=pltpu.VMEM)] * 4,
        out_specs=(pl.BlockSpec(memory_space=pltpu.VMEM), pl.BlockSpec(memory_space=pltpu.VMEM)),
        scratch_shapes=[
            vmem(groups, inner, span),
            pltpu.VMEM((2 * rows, inner), BF16),
            vmem(inner, 128),
            vmem(2 * nb, rows),
            vmem(groups, rows, 128),
            vmem(n, 2 * nb, wide),
            vmem(n, nb, wide),
            vmem(n, nb, wide),
            vmem(n, 3, nb // 4, wide),
            vmem(n, nb // 4, wide),
            vmem(n, 3, nb // 16, wide),
            vmem(n, nb // 16, wide),
            vmem(n, 4, nb // 16, wide),
            vmem(n, 2 * nb, wide),
            vmem(2 * nb, inner),
            sems((len(OFFSETS), HALVES)),
            sems((len(OFFSETS), HALVES)),
            sems((len(OFFSETS), HALVES)),
            sems((len(OFFSETS), HALVES)),
            sems((2,)),
            sems((groups,)),
            sems((groups - 1,)),
            sems((groups - 1,)),
            sems((n, 17)),
            sems((n, 17)),
        ],
        compiler_params=pltpu.CompilerParams(
            collective_id=0, has_side_effects=True, vmem_limit_bytes=54 * 2**20
        ),
        cost_estimate=pl.CostEstimate(
            flops=6 * rows * inner * cols, bytes_accessed=4 * rows * cols, transcendentals=0
        ),
    )(merge_coef, basis, panels, factors)


def solution(mesh):
    return jax.shard_map(
        per_device,
        mesh=mesh,
        in_specs=(P("row", "col"), P("row", "col"), P(None, ("row", "col"), None), P()),
        out_specs=(P(("row", "col"), None), P()),
        check_vma=False,
    )
```
